32 devices in a mesh: groups: 2 (over y), dp: 4 (over z), tensor: 4 (over x, core).
Axes of the slice: x: 2, y: 2, z: 4, core: 2. Of those that a mesh axis runs over, the one named last changes fastest.
Arguments:
- train_rows: bfloat16 [2048, 5120], P(('groups', 'dp')), parts along dimension 0, may hold values from -40 to 40
- out_grads: bfloat16 [2048, 27648], P(('groups', 'dp'), 'tensor'), parts along dimension 0, may hold values from -6 to 6
- input_factor: bfloat16 [512, 5120], P(('groups', 'dp'), 'tensor'), parts along dimension 0, may hold values from -0.078125 to 0.078125
- output_factor: bfloat16 [512, 27648], P(('groups', 'dp'), 'tensor'), parts along dimension 0, may hold values from -0.0068359375 to 0.0068359375
- train_ids: int32 [2048], P(('groups', 'dp')), parts along dimension 0, may hold values from 0 to 100351
- query_ids: int32 [16], P('groups'), parts along dimension 0, may hold values from 0 to 100351
- loss_weights: float32 [100352], replicated, may hold values from 0.3 to 3
Outputs:
- scores: float32 [8, 2048], P(None, ('groups', 'dp', 'tensor')), parts along dimension 1
The draws below stay inside these ranges and needn't reach their ends.
There are 2 independent parts, one for each index of `groups`. The reference program is written for one: setup_inputs(seed, part) draws one part's arguments, and reference() takes and returns one part's arrays. A program takes and returns all parts, laid end to end along the dimension named above; an argument that names none is the same for every part. Nothing has to cross between parts.
All inputs are finite; a program needn't handle non-finite values.
Results may differ from the reference program's by a relative error of at most 0.0003.
Values may be sent and summed in bfloat16 or wider, within the bound.
A program may use at most 128 MiB of HBM per device.

```python
import math
import jax
import jax.numpy as jnp
import numpy as np

D = 5120
FF = 27648
VOCAB = 100352
RANK = 32
TOKENS = 1024
QUERIES = 8
QROWS = 256


def draw_train_rows(key, part):
    key = jax.random.fold_in(key, 11)
    key_base, key_rows, key_cols = jax.random.split(key, 3)
    row_scale = jnp.exp(jax.random.uniform(key_rows, (TOKENS, 1), jnp.float32) * math.log(10.0))
    col_scale = 0.1 * jnp.exp(jax.random.uniform(key_cols, (1, D), jnp.float32) * math.log(10.0))
    base = jax.random.truncated_normal(key_base, -4.0, 4.0, (TOKENS, D), jnp.float32)
    return (base * row_scale * col_scale).astype(jnp.bfloat16)


def touch_ends(array, rng, smallest, high):
    longest = array.shape.index(max(array.shape))
    spots = []
    for shift in (0, 1):
        where = [jax.random.randint(jax.random.fold_in(rng, axis), (), 0, length) for axis, length in enumerate(array.shape)]
        where[longest] = (where[longest] + shift) % array.shape[longest]
        spots.append(tuple(where))
    return array.at[spots[0]].set(smallest).at[spots[1]].set(high)


def level_of(key, extent, cuts, least, largest):
    gain, own = 1.0, jax.random.fold_in(key, 6)
    for dim, parts in cuts:
        heights = jnp.exp(jax.random.uniform(jax.random.fold_in(own, dim), (parts,), jnp.float32, least / len(cuts), largest / len(cuts)))
        gain = gain * jnp.repeat(heights, extent[dim] // parts).reshape([-1 if axis == dim else 1 for axis in range(len(extent))])
    return gain


def wide_ids(rng, extent, amount, skew):
    portions = [min(1 << octave, amount + 1 - (1 << octave)) * (1 << 20) // math.isqrt((1 << octave) ** skew) + 1 for octave in range((amount + 1).bit_length()) if 1 << octave <= amount]
    deviation = 1 + sum(portions) // (1 << 30)
    grid = np.cumsum(np.array([max(1, weight // deviation) for weight in portions]))
    pick = jax.random.randint(jax.random.fold_in(rng, 1), extent, 0, int(grid[len(portions) - 1]))
    start = jnp.left_shift(1, jnp.searchsorted(jnp.asarray(grid, jnp.int32), pick, side="right").astype(jnp.int32))
    grade = start - 1 + jax.random.randint(jax.random.fold_in(rng, 4), extent, 0, 1 << 30) % jnp.minimum(start, amount + 1 - start)
    return jax.random.permutation(jax.random.fold_in(rng, 2), amount)[grade].astype(jnp.int32)


def bell_draw(stream_key, shape, deviation, limit, shards=(), dtype=jnp.bfloat16):
    loudness = level_of(stream_key, shape, shards, -0.22, 0.18) if shards else 1.0
    values = jax.random.normal(stream_key, shape, jnp.float32) * deviation * loudness
    return jnp.minimum(jnp.maximum(values, -limit), limit).astype(dtype)


def setup_inputs(seed: int = 0, part: int = 0) -> dict:
    arg_keys = jax.random.split(jax.random.key(seed), 8)
    part_splits = jax.random.split(jax.random.fold_in(arg_keys[7], part), 8)
    train_rows = draw_train_rows(jax.random.fold_in(jax.random.fold_in(arg_keys[7], part), 71), part)
    out_grads = bell_draw(part_splits[1], (TOKENS, FF), 1.0, 6.0, ((0, 4), (1, 4)))
    input_factor = bell_draw(part_splits[2], (QROWS, D), D ** -0.5, 0.078125, ((0, 4), (1, 4)))
    output_factor = bell_draw(part_splits[3], (QROWS, FF), (FF * RANK) ** -0.5, 0.0068359375, ((0, 4), (1, 4)))
    train_ids = touch_ends(wide_ids(part_splits[4], (TOKENS,), VOCAB, 2), jax.random.fold_in(part_splits[4], 3), 0, VOCAB - 1).astype(jnp.int32)
    query_ids = touch_ends(jax.random.randint(part_splits[5], (QUERIES,), 0, VOCAB), jax.random.fold_in(part_splits[5], 1), 0, VOCAB - 1).astype(jnp.int32)
    loss_weights = jnp.clip(jnp.exp(jax.random.uniform(arg_keys[6], (VOCAB,), jnp.float32, math.log(0.3), math.log(3.0))), 0.3, 3.0)
    return dict(train_rows=train_rows, out_grads=out_grads, input_factor=input_factor, output_factor=output_factor, train_ids=train_ids, query_ids=query_ids, loss_weights=loss_weights)


def reference(train_rows, out_grads, input_factor, output_factor, train_ids, query_ids, loss_weights):
    input_proj = jnp.dot(train_rows, input_factor.T, preferred_element_type=jnp.float32)
    grad_proj = jnp.dot(out_grads, output_factor.T, preferred_element_type=jnp.float32)
    raw_scores = (input_proj * grad_proj).reshape(TOKENS, QUERIES, RANK).sum(axis=2)
    tok_weight = loss_weights[train_ids]
    query_weight = loss_weights[query_ids]
    return (raw_scores * tok_weight[:, None] * query_weight[None, :]).T
```

```python
import functools

import jax
import jax.numpy as jnp
from jax import lax
from jax.experimental import pallas as pl
from jax.experimental.pallas import tpu as pltpu
from jax.sharding import PartitionSpec as P

LANES = 128
CHUNK_ROWS = 16
K_TILE = 768


def contract(left, right):
    return lax.dot_general(left, right, (((1,), (1,)), ((), ())), preferred_element_type=jnp.float32)


def kernel(
    n, ways, rank_count,
    rows_ref, grads_ref, in_ref, out_factor_ref, table_ref, ids_ref, query_ids_ref,
    scores_ref,
    x_buf, g_buf, in_buf, of_buf, table_buf, proj, landed, tok_buf, query_buf,
    local_sem, in_send, in_recv, of_send, of_recv, sum_send, sum_recv,
):
    place = lax.axis_index("dp")
    tensor_place = lax.axis_index("tensor")
    factor_rows, width = in_ref.shape
    hidden = out_factor_ref.shape[1]
    queries = query_ids_ref.shape[0]
    share = scores_ref.shape[1]
    chunks = factor_rows // CHUNK_ROWS
    has_left = place > 0
    has_right = place < n - 1

    local = [
        pltpu.make_async_copy(grads_ref, g_buf, local_sem.at[0]),
        pltpu.make_async_copy(
            rows_ref.at[:, pl.ds(pl.multiple_of(tensor_place * width, LANES), width)], x_buf, local_sem.at[1]
        ),
        pltpu.make_async_copy(out_factor_ref, of_buf.at[place], local_sem.at[2]),
        pltpu.make_async_copy(in_ref, in_buf.at[place], local_sem.at[3]),
        pltpu.make_async_copy(table_ref, table_buf, local_sem.at[4]),
    ]

    barrier = pltpu.get_barrier_semaphore()

    @pl.when(has_left)
    def _():
        pl.semaphore_signal(barrier, inc=1, device_id={"dp": place - 1}, device_id_type=pl.DeviceIdType.MESH)

    @pl.when(has_right)
    def _():
        pl.semaphore_signal(barrier, inc=1, device_id={"dp": place + 1}, device_id_type=pl.DeviceIdType.MESH)

    for step in range(1, ways):
        pl.semaphore_signal(
            barrier, inc=1, device_id={"tensor": lax.rem(tensor_place + step, ways)},
            device_id_type=pl.DeviceIdType.MESH,
        )
    neighbours = jnp.where(has_left, 1, 0) + jnp.where(has_right, 1, 0)
    pl.semaphore_wait(barrier, neighbours + (ways - 1))

    def hop(way, hops, chunk, slab, own=False):
        target = {"dp": place + (1 if way == 0 else -1)}
        if chunk == chunks:
            return pltpu.make_async_remote_copy(
                src_ref=in_ref if own else in_buf.at[slab], dst_ref=in_buf.at[slab],
                send_sem=in_send.at[way, hops], recv_sem=in_recv.at[way, hops],
                device_id=target, device_id_type=pl.DeviceIdType.MESH,
            )
        band = pl.ds(chunk * CHUNK_ROWS, CHUNK_ROWS)
        return pltpu.make_async_remote_copy(
            src_ref=out_factor_ref.at[band, :] if own else of_buf.at[slab, band, :], dst_ref=of_buf.at[slab, band, :],
            send_sem=of_send.at[way, hops, chunk], recv_sem=of_recv.at[way, hops, chunk],
            device_id=target, device_id_type=pl.DeviceIdType.MESH,
        )

    for chunk in range(chunks + 1):
        @pl.when(has_right)
        def _():
            hop(0, 0, chunk, place, own=True).start()

        @pl.when(has_left)
        def _():
            hop(1, 0, chunk, place, own=True).start()

    for copy in local:
        copy.start()

    def to_peer(slab, step):
        peer = lax.rem(tensor_place + step, ways)
        return pltpu.make_async_remote_copy(
            src_ref=proj.at[slab, pl.ds(pl.multiple_of(peer * share, 8), share), :],
            dst_ref=landed.at[slab, step - 1],
            send_sem=sum_send.at[slab, step - 1], recv_sem=sum_recv.at[slab, step - 1],
            device_id={"tensor": peer}, device_id_type=pl.DeviceIdType.MESH,
        )

    def project(slab):
        tokens = g_buf.shape[0]

        def tile(index, total):
            columns = pl.ds(pl.multiple_of(index * K_TILE, LANES), K_TILE)
            return total + contract(g_buf[:, columns], of_buf[slab, :, columns])

        grad = lax.fori_loop(0, hidden // K_TILE, tile, jnp.zeros((tokens, factor_rows), jnp.float32))
        proj[slab, :, 0:factor_rows] = contract(x_buf[...], in_buf[slab])
        proj[slab, :, factor_rows:2 * factor_rows] = grad
        for step in range(1, ways):
            to_peer(slab, step).start()

    for copy in local:
        copy.wait()
    project(place)

    lane = lax.broadcasted_iota(jnp.int32, (1, LANES), 1)

    def pick(ids, base, into):
        def body(index, carry):
            number = ids[base + index]
            row = table_buf[pl.ds(lax.shift_right_logical(number, 7), 1), :]
            into[pl.ds(index, 1), :] = jnp.where(lane == jnp.bitwise_and(number, LANES - 1), row, 0.0)
            return carry
        return body

    lax.fori_loop(0, share, pick(ids_ref, tensor_place * share, tok_buf), 0)
    lax.fori_loop(0, queries, pick(query_ids_ref, 0, query_buf), 0)

    def arrive(step, carry):
        from_left = place - 1 - step
        from_right = place + 1 + step
        for chunk in range(chunks + 1):
            @pl.when(from_left >= 0)
            def _():
                hop(0, step, chunk, from_left).wait_recv()

                @pl.when(has_right)
                def _():
                    hop(0, step + 1, chunk, from_left).start()

            @pl.when(from_right < n)
            def _():
                hop(1, step, chunk, from_right).wait_recv()

                @pl.when(has_left)
                def _():
                    hop(1, step + 1, chunk, from_right).start()

        @pl.when(from_left >= 0)
        def _():
            project(from_left)

        @pl.when(from_right < n)
        def _():
            project(from_right)

        return carry

    lax.fori_loop(0, n - 1, arrive, 0)

    tok_weight = jnp.sum(tok_buf[...], axis=1, keepdims=True)
    query_weight = jnp.sum(query_buf[...], axis=1, keepdims=True)
    which = lax.broadcasted_iota(jnp.int32, (queries, LANES), 0)
    where = lax.broadcasted_iota(jnp.int32, (queries, LANES), 1)

    def finish(slab, scores):
        total = proj[slab, pl.ds(pl.multiple_of(tensor_place * share, 8), share), :]
        for step in range(1, ways):
            to_peer(slab, step).wait_recv()
            total = total + landed[slab, step - 1]
        product = total * pltpu.roll(total, factor_rows, 1)
        first = which * rank_count - slab * factor_rows
        chosen = (where >= first) & (where < first + rank_count) & (where < factor_rows)
        return scores + lax.dot_general(
            jnp.where(chosen, 1.0, 0.0), product * tok_weight, (((1,), (1,)), ((), ())),
            precision=lax.Precision.HIGHEST, preferred_element_type=jnp.float32,
        )

    scores = lax.fori_loop(0, n, finish, jnp.zeros((queries, share), jnp.float32))
    scores_ref[...] = scores * query_weight

    def drain(step, carry):
        for chunk in range(chunks + 1):
            @pl.when(has_right & (step <= place))
            def _():
                hop(0, step, chunk, place - step).wait_send()

            @pl.when(has_left & (place + step < n))
            def _():
                hop(1, step, chunk, place + step).wait_send()
        for offset in range(1, ways):
            to_peer(step, offset).wait_send()
        return carry

    lax.fori_loop(0, n, drain, 0)


def solution(mesh):
    n, ways = mesh.shape["dp"], mesh.shape["tensor"]

    def shards(train_rows, out_grads, input_factor, output_factor, train_ids, query_ids, loss_weights):
        tokens, hidden = out_grads.shape
        factor_rows, width = input_factor.shape
        queries = query_ids.shape[0]
        share = tokens // ways
        chunks = factor_rows // CHUNK_ROWS
        rank_count = factor_rows * n // queries
        table = loss_weights.reshape(-1, LANES)
        anywhere = pl.BlockSpec(memory_space=pl.ANY)
        scalars = pl.BlockSpec(memory_space=pltpu.SMEM)
        dma = pltpu.SemaphoreType.DMA
        return pl.pallas_call(
            functools.partial(kernel, n, ways, rank_count),
            out_shape=jax.ShapeDtypeStruct((queries, share), jnp.float32),
            in_specs=[anywhere] * 5 + [scalars] * 2,
            out_specs=pl.BlockSpec(memory_space=pltpu.VMEM),
            scratch_shapes=[
                pltpu.VMEM((tokens, width), jnp.bfloat16),
                pltpu.VMEM((tokens, hidden), jnp.bfloat16),
                pltpu.VMEM((n, factor_rows, width), jnp.bfloat16),
                pltpu.VMEM((n, factor_rows, hidden), jnp.bfloat16),
                pltpu.VMEM(table.shape, jnp.float32),
                pltpu.VMEM((n, tokens, 2 * factor_rows), jnp.float32),
                pltpu.VMEM((n, ways - 1, share, 2 * factor_rows), jnp.float32),
                pltpu.VMEM((share, LANES), jnp.float32),
                pltpu.VMEM((queries, LANES), jnp.float32),
                dma((5,)),
                dma((2, n)), dma((2, n)),
                dma((2, n, chunks)), dma((2, n, chunks)),
                dma((n, ways - 1)), dma((n, ways - 1)),
            ],
            compiler_params=pltpu.CompilerParams(
                collective_id=0, has_side_effects=True, vmem_limit_bytes=56 * 2**20
            ),
        )(train_rows, out_grads, input_factor, output_factor, table, train_ids, query_ids)

    return jax.shard_map(
        shards,
        mesh=mesh,
        in_specs=(
            P(("groups", "dp"), None),
            P(("groups", "dp"), "tensor"),
            P(("groups", "dp"), "tensor"),
            P(("groups", "dp"), "tensor"),
            P(("groups", "dp")),
            P("groups"),
            P(),
        ),
        out_specs=P(None, ("groups", "dp", "tensor")),
        check_vma=False,
    )
```

```python
import functools

import jax
import jax.numpy as jnp
from jax import lax
from jax.experimental import pallas as pl
from jax.experimental.pallas import tpu as pltpu
from jax.sharding import PartitionSpec as P

LANES = 128
MOVED_PART = 3 / 8
MOVED_CHUNKS = 2
KEPT_CHUNKS = 4


def contract(left, right):
    return lax.dot_general(left, right, (((1,), (1,)), ((), ())), preferred_element_type=jnp.float32)


def column_chunks(hidden, moved):
    def cut(low, high, parts):
        tiles = (high - low) // LANES
        marks = [low + (tiles * part // parts) * LANES for part in range(parts)] + [high]
        return [(begin, end - begin) for begin, end in zip(marks[:-1], marks[1:])]

    first = cut(hidden - moved, hidden, MOVED_CHUNKS) if moved else []
    return first, cut(0, hidden - moved, KEPT_CHUNKS)


def kernel(
    n, ways, rank_count, moved,
    rows_ref, grads_ref, in_ref, out_factor_ref, table_ref, ids_ref, query_ids_ref,
    scores_ref,
    x_buf, g_buf, in_buf, of_buf, table_buf, acc, proj, landed, tok_buf, query_buf,
    guest, guest_proj, extra,
    local_sem, in_send, in_recv, of_send, of_recv, sum_send, sum_recv,
    guest_send, guest_recv, extra_send, extra_recv,
):
    place = lax.axis_index("dp")
    tensor_place = lax.axis_index("tensor")
    factor_rows, width = in_ref.shape
    hidden = out_factor_ref.shape[1]
    queries = query_ids_ref.shape[0]
    share = scores_ref.shape[1]
    kept = hidden - moved
    moved_chunks, kept_chunks = column_chunks(hidden, moved)
    chunks = moved_chunks + [None] + kept_chunks
    has_left = place > 0
    has_right = place < n - 1
    at_end = (place == 0) | (place == n - 1)
    hosting = (place == 1) | (place == n - 2)
    guest_place = jnp.where(place == 1, 0, n - 1)
    host_place = jnp.where(place == 0, 1, n - 2)
    mesh_ids = pl.DeviceIdType.MESH

    local = [
        pltpu.make_async_copy(grads_ref, g_buf, local_sem.at[0]),
        pltpu.make_async_copy(
            rows_ref.at[:, pl.ds(pl.multiple_of(tensor_place * width, LANES), width)], x_buf, local_sem.at[1]
        ),
        pltpu.make_async_copy(out_factor_ref, of_buf.at[place], local_sem.at[2]),
        pltpu.make_async_copy(in_ref, in_buf.at[place], local_sem.at[3]),
        pltpu.make_async_copy(table_ref, table_buf, local_sem.at[4]),
    ]

    barrier = pltpu.get_barrier_semaphore()

    @pl.when(has_left)
    def _():
        pl.semaphore_signal(barrier, inc=1, device_id={"dp": place - 1}, device_id_type=mesh_ids)

    @pl.when(has_right)
    def _():
        pl.semaphore_signal(barrier, inc=1, device_id={"dp": place + 1}, device_id_type=mesh_ids)

    for step in range(1, ways):
        peer = lax.rem(tensor_place + step, ways)
        pl.semaphore_signal(barrier, inc=1, device_id={"tensor": peer}, device_id_type=mesh_ids)
        if moved:
            @pl.when(at_end)
            def _():
                pl.semaphore_signal(
                    barrier, inc=1, device_id={"dp": host_place, "tensor": peer}, device_id_type=mesh_ids
                )
    greeters = jnp.where(has_left, 1, 0) + jnp.where(has_right, 1, 0) + (ways - 1)
    if moved:
        greeters = greeters + jnp.where(hosting, ways - 1, 0)
    pl.semaphore_wait(barrier, greeters)

    def hop(way, hops, chunk, slab, own=False):
        target = {"dp": place + (1 if way == 0 else -1)}
        if chunks[chunk] is None:
            return pltpu.make_async_remote_copy(
                src_ref=in_ref if own else in_buf.at[slab], dst_ref=in_buf.at[slab],
                send_sem=in_send.at[way, hops], recv_sem=in_recv.at[way, hops],
                device_id=target, device_id_type=mesh_ids,
            )
        begin, size = chunks[chunk]
        columns = pl.ds(begin, size)
        return pltpu.make_async_remote_copy(
            src_ref=out_factor_ref.at[:, columns] if own else of_buf.at[slab, :, columns],
            dst_ref=of_buf.at[slab, :, columns],
            send_sem=of_send.at[way, hops, chunk], recv_sem=of_recv.at[way, hops, chunk],
            device_id=target, device_id_type=mesh_ids,
        )

    def sends(way, chunk):
        if chunk < len(moved_chunks):
            return place < n - 2 if way == 0 else place > 1
        return has_right if way == 0 else has_left

    def takes(way, chunk, slab):
        valid = slab >= 0 if way == 0 else slab < n
        if chunk < len(moved_chunks):
            return valid & jnp.logical_not(at_end)
        return valid

    def lend(band):
        rows = pl.ds(band * share, share)
        return pltpu.make_async_remote_copy(
            src_ref=grads_ref.at[rows, pl.ds(kept, moved)], dst_ref=guest.at[rows, :],
            send_sem=guest_send.at[band], recv_sem=guest_recv.at[band],
            device_id={"dp": host_place}, device_id_type=mesh_ids,
        )

    def hand_back(band, source):
        return pltpu.make_async_remote_copy(
            src_ref=guest_proj.at[band], dst_ref=extra.at[source],
            send_sem=extra_send.at[band], recv_sem=extra_recv.at[source],
            device_id={"dp": guest_place, "tensor": band}, device_id_type=mesh_ids,
        )

    for chunk in range(len(chunks)):
        for way in range(2):
            @pl.when(sends(way, chunk))
            def _():
                hop(way, 0, chunk, place, own=True).start()

    if moved:
        @pl.when(at_end)
        def _():
            for band in range(ways):
                lend(band).start()

    for copy in local:
        copy.start()

    def to_peer(slab, step):
        peer = lax.rem(tensor_place + step, ways)
        return pltpu.make_async_remote_copy(
            src_ref=proj.at[slab, pl.ds(pl.multiple_of(peer * share, 8), share), :],
            dst_ref=landed.at[slab, step - 1],
            send_sem=sum_send.at[slab, step - 1], recv_sem=sum_recv.at[slab, step - 1],
            device_id={"tensor": peer}, device_id_type=mesh_ids,
        )

    def add_chunk(way, chunk, slab):
        if chunks[chunk] is None:
            proj[slab, :, 0:factor_rows] = contract(x_buf[...], in_buf[slab])
        else:
            begin, size = chunks[chunk]
            acc[way] += contract(g_buf[:, begin:begin + size], of_buf[slab, :, begin:begin + size])

    def send_sums(way, slab):
        proj[slab, :, factor_rows:2 * factor_rows] = acc[way]
        for step in range(1, ways):
            to_peer(slab, step).start()

    acc[...] = jnp.zeros_like(acc)
    for copy in local:
        copy.wait()
    for chunk in range(len(chunks)):
        if chunk < len(moved_chunks):
            @pl.when(jnp.logical_not(at_end))
            def _():
                add_chunk(0, chunk, place)
        else:
            add_chunk(0, chunk, place)
    send_sums(0, place)

    lane = lax.broadcasted_iota(jnp.int32, (1, LANES), 1)

    def pick(ids, base, into):
        def body(index, carry):
            number = ids[base + index]
            row = table_buf[pl.ds(lax.shift_right_logical(number, 7), 1), :]
            into[pl.ds(index, 1), :] = jnp.where(lane == jnp.bitwise_and(number, LANES - 1), row, 0.0)
            return carry
        return body

    lax.fori_loop(0, share, pick(ids_ref, tensor_place * share, tok_buf), 0)
    lax.fori_loop(0, queries, pick(query_ids_ref, 0, query_buf), 0)

    def arrive(step, carry):
        slabs = (place - 1 - step, place + 1 + step)
        acc[...] = jnp.zeros_like(acc)
        for chunk in range(len(chunks)):
            for way in range(2):
                @pl.when(takes(way, chunk, slabs[way]))
                def _():
                    hop(way, step, chunk, slabs[way]).wait_recv()

                    @pl.when(sends(way, chunk))
                    def _():
                        hop(way, step + 1, chunk, slabs[way]).start()

                    add_chunk(way, chunk, slabs[way])
                    if chunk == len(chunks) - 1:
                        send_sums(way, slabs[way])
        return carry

    lax.fori_loop(0, n - 1, arrive, 0)

    if moved:
        @pl.when(hosting)
        def _():
            for band in range(ways):
                lend(band).wait_recv()
                tokens = guest[band * share:(band + 1) * share, :]

                def pair(index, carry):
                    factors = of_buf[pl.ds(index * 2, 2), :, kept:hidden].reshape(2 * factor_rows, moved)
                    guest_proj[band, index] = contract(tokens, factors)
                    return carry

                lax.fori_loop(0, n // 2, pair, 0)
                hand_back(band, tensor_place).start()

    tok_weight = jnp.sum(tok_buf[...], axis=1, keepdims=True)
    query_weight = jnp.sum(query_buf[...], axis=1, keepdims=True)
    which = lax.broadcasted_iota(jnp.int32, (queries, LANES), 0)
    where = lax.broadcasted_iota(jnp.int32, (queries, LANES), 1)

    def finish(slab, scores):
        total = proj[slab, pl.ds(pl.multiple_of(tensor_place * share, 8), share), :]
        for step in range(1, ways):
            to_peer(slab, step).wait_recv()
            total = total + landed[slab, step - 1]
        proj[slab, pl.ds(pl.multiple_of(tensor_place * share, 8), share), :] = total
        return scores

    lax.fori_loop(0, n, finish, 0)

    if moved:
        @pl.when(at_end)
        def _():
            for source in range(ways):
                hand_back(tensor_place, source).wait_recv()

            def add_extra(slab, carry):
                pair = lax.div(slab, 2)
                more = extra[0, pair]
                for source in range(1, ways):
                    more = more + extra[source, pair]
                more = jnp.where(lax.rem(slab, 2) == 0, pltpu.roll(more, factor_rows, 1), more)
                rows = pl.ds(pl.multiple_of(tensor_place * share, 8), share)
                proj[slab, rows, :] += jnp.where(lane >= factor_rows, more, 0.0)
                return carry

            lax.fori_loop(0, n, add_extra, 0)

    def score(slab, scores):
        total = proj[slab, pl.ds(pl.multiple_of(tensor_place * share, 8), share), :]
        product = total * pltpu.roll(total, factor_rows, 1)
        first = which * rank_count - slab * factor_rows
        chosen = (where >= first) & (where < first + rank_count) & (where < factor_rows)
        chosen = chosen & (first >= 0)
        return scores + lax.dot_general(
            jnp.where(chosen, 1.0, 0.0), product * tok_weight, (((1,), (1,)), ((), ())),
            precision=lax.Precision.HIGHEST, preferred_element_type=jnp.float32,
        )

    scores = lax.fori_loop(0, n, score, jnp.zeros((queries, share), jnp.float32))
    scores_ref[...] = scores * query_weight

    def drain(step, carry):
        for chunk in range(len(chunks)):
            for way in range(2):
                slab = place - step if way == 0 else place + step
                @pl.when(sends(way, chunk) & ((slab >= 0) & (slab < n)))
                def _():
                    hop(way, step, chunk, slab).wait_send()
        for offset in range(1, ways):
            to_peer(step, offset).wait_send()
        return carry

    lax.fori_loop(0, n, drain, 0)

    if moved:
        @pl.when(at_end)
        def _():
            for band in range(ways):
                lend(band).wait_send()

        @pl.when(hosting)
        def _():
            for band in range(ways):
                hand_back(band, tensor_place).wait_send()


def solution(mesh):
    n, ways = mesh.shape["dp"], mesh.shape["tensor"]

    def shards(train_rows, out_grads, input_factor, output_factor, train_ids, query_ids, loss_weights):
        tokens, hidden = out_grads.shape
        factor_rows, width = input_factor.shape
        queries = query_ids.shape[0]
        share = tokens // ways
        moved = int(hidden // LANES * MOVED_PART) * LANES if n >= 4 and n % 2 == 0 else 0
        count = sum(len(part) for part in column_chunks(hidden, moved)) + 1
        rank_count = factor_rows * n // queries
        table = loss_weights.reshape(-1, LANES)
        anywhere = pl.BlockSpec(memory_space=pl.ANY)
        scalars = pl.BlockSpec(memory_space=pltpu.SMEM)
        dma = pltpu.SemaphoreType.DMA
        pairs = (ways, max(n // 2, 1), share, 2 * factor_rows)
        return pl.pallas_call(
            functools.partial(kernel, n, ways, rank_count, moved),
            out_shape=jax.ShapeDtypeStruct((queries, share), jnp.float32),
            in_specs=[anywhere] * 5 + [scalars] * 2,
            out_specs=pl.BlockSpec(memory_space=pltpu.VMEM),
            scratch_shapes=[
                pltpu.VMEM((tokens, width), jnp.bfloat16),
                pltpu.VMEM((tokens, hidden), jnp.bfloat16),
                pltpu.VMEM((n, factor_rows, width), jnp.bfloat16),
                pltpu.VMEM((n, factor_rows, hidden), jnp.bfloat16),
                pltpu.VMEM(table.shape, jnp.float32),
                pltpu.VMEM((2, tokens, factor_rows), jnp.float32),
                pltpu.VMEM((n, tokens, 2 * factor_rows), jnp.float32),
                pltpu.VMEM((n, ways - 1, share, 2 * factor_rows), jnp.float32),
                pltpu.VMEM((share, LANES), jnp.float32),
                pltpu.VMEM((queries, LANES), jnp.float32),
                pltpu.VMEM((tokens, max(moved, LANES)), jnp.bfloat16),
                pltpu.VMEM(pairs, jnp.float32),
                pltpu.VMEM(pairs, jnp.float32),
                dma((5,)),
                dma((2, n)), dma((2, n)),
                dma((2, n, count)), dma((2, n, count)),
                dma((n, ways - 1)), dma((n, ways - 1)),
                dma((ways,)), dma((ways,)), dma((ways,)), dma((ways,)),
            ],
            compiler_params=pltpu.CompilerParams(
                collective_id=0, has_side_effects=True, vmem_limit_bytes=58 * 2**20
            ),
        )(train_rows, out_grads, input_factor, output_factor, table, train_ids, query_ids)

    return jax.shard_map(
        shards,
        mesh=mesh,
        in_specs=(
            P(("groups", "dp"), None),
            P(("groups", "dp"), "tensor"),
            P(("groups", "dp"), "tensor"),
            P(("groups", "dp"), "tensor"),
            P(("groups", "dp")),
            P("groups"),
            P(),
        ),
        out_specs=P(None, ("groups", "dp", "tensor")),
        check_vma=False,
    )
```

```python
import functools

import jax
import jax.numpy as jnp
from jax import lax
from jax.experimental import pallas as pl
from jax.experimental.pallas import tpu as pltpu
from jax.sharding import PartitionSpec as P

LANES = 128
MOVED_PART = 5 / 16
MOVED_CHUNKS = 2
KEPT_CHUNKS = 4


def contract(left, right):
    return lax.dot_general(left, right, (((1,), (1,)), ((), ())), preferred_element_type=jnp.float32)


def column_chunks(hidden, moved):
    def cut(low, high, parts):
        tiles = (high - low) // LANES
        marks = [low + (tiles * part // parts) * LANES for part in range(parts)] + [high]
        return [(begin, end - begin) for begin, end in zip(marks[:-1], marks[1:])]

    first = cut(hidden - moved, hidden, MOVED_CHUNKS) if moved else []
    return first, cut(0, hidden - moved, KEPT_CHUNKS)


def kernel(
    n, ways, rank_count, moved,
    rows_ref, grads_ref, in_ref, out_factor_ref, table_ref, ids_ref, query_ids_ref,
    scores_ref, query_weight_ref,
    x_buf, g_buf, in_buf, of_buf, table_buf, acc, proj, landed, tok_buf, query_buf,
    guest, guest_proj, extra,
    local_sem, in_send, in_recv, of_send, of_recv, sum_send, sum_recv,
    guest_send, guest_recv, extra_send, extra_recv,
):
    place = lax.axis_index("dp")
    tensor_place = lax.axis_index("tensor")
    factor_rows, width = in_ref.shape
    hidden = out_factor_ref.shape[1]
    queries = query_ids_ref.shape[0]
    share = scores_ref.shape[1]
    kept = hidden - moved
    moved_chunks, kept_chunks = column_chunks(hidden, moved)
    chunks = moved_chunks + [None] + kept_chunks
    has_left = place > 0
    has_right = place < n - 1
    at_end = (place == 0) | (place == n - 1)
    hosting = (place == 1) | (place == n - 2)
    guest_place = jnp.where(place == 1, 0, n - 1)
    host_place = jnp.where(place == 0, 1, n - 2)
    mesh_ids = pl.DeviceIdType.MESH

    local = [
        pltpu.make_async_copy(grads_ref, g_buf, local_sem.at[0]),
        pltpu.make_async_copy(
            rows_ref.at[:, pl.ds(pl.multiple_of(tensor_place * width, LANES), width)], x_buf, local_sem.at[1]
        ),
        pltpu.make_async_copy(out_factor_ref, of_buf.at[place], local_sem.at[2]),
        pltpu.make_async_copy(in_ref, in_buf.at[place], local_sem.at[3]),
        pltpu.make_async_copy(table_ref, table_buf, local_sem.at[4]),
    ]

    barrier = pltpu.get_barrier_semaphore()

    @pl.when(has_left)
    def _():
        pl.semaphore_signal(barrier, inc=1, device_id={"dp": place - 1}, device_id_type=mesh_ids)

    @pl.when(has_right)
    def _():
        pl.semaphore_signal(barrier, inc=1, device_id={"dp": place + 1}, device_id_type=mesh_ids)

    for step in range(1, ways):
        peer = lax.rem(tensor_place + step, ways)
        pl.semaphore_signal(barrier, inc=1, device_id={"tensor": peer}, device_id_type=mesh_ids)
        if moved:
            @pl.when(at_end)
            def _():
                pl.semaphore_signal(
                    barrier, inc=1, device_id={"dp": host_place, "tensor": peer}, device_id_type=mesh_ids
                )
    greeters = jnp.where(has_left, 1, 0) + jnp.where(has_right, 1, 0) + (ways - 1)
    if moved:
        greeters = greeters + jnp.where(hosting, ways - 1, 0)
    pl.semaphore_wait(barrier, greeters)

    def hop(way, hops, chunk, slab, own=False):
        target = {"dp": place + (1 if way == 0 else -1)}
        if chunks[chunk] is None:
            return pltpu.make_async_remote_copy(
                src_ref=in_ref if own else in_buf.at[slab], dst_ref=in_buf.at[slab],
                send_sem=in_send.at[way, hops], recv_sem=in_recv.at[way, hops],
                device_id=target, device_id_type=mesh_ids,
            )
        begin, size = chunks[chunk]
        columns = pl.ds(begin, size)
        return pltpu.make_async_remote_copy(
            src_ref=out_factor_ref.at[:, columns] if own else of_buf.at[slab, :, columns],
            dst_ref=of_buf.at[slab, :, columns],
            send_sem=of_send.at[way, hops, chunk], recv_sem=of_recv.at[way, hops, chunk],
            device_id=target, device_id_type=mesh_ids,
        )

    def sends(way, chunk):
        if chunk < len(moved_chunks):
            return place < n - 2 if way == 0 else place > 1
        return has_right if way == 0 else has_left

    def takes(way, chunk, slab):
        valid = slab >= 0 if way == 0 else slab < n
        if chunk < len(moved_chunks):
            return valid & jnp.logical_not(at_end)
        return valid

    def lend(band):
        rows = pl.ds(band * share, share)
        return pltpu.make_async_remote_copy(
            src_ref=grads_ref.at[rows, pl.ds(kept, moved)], dst_ref=guest.at[rows, :],
            send_sem=guest_send.at[band], recv_sem=guest_recv.at[band],
            device_id={"dp": host_place}, device_id_type=mesh_ids,
        )

    def hand_back(band, source):
        return pltpu.make_async_remote_copy(
            src_ref=guest_proj.at[band], dst_ref=extra.at[source],
            send_sem=extra_send.at[band], recv_sem=extra_recv.at[source],
            device_id={"dp": guest_place, "tensor": band}, device_id_type=mesh_ids,
        )

    for chunk in range(len(chunks)):
        for way in range(2):
            @pl.when(sends(way, chunk))
            def _():
                hop(way, 0, chunk, place, own=True).start()

    if moved:
        @pl.when(at_end)
        def _():
            for band in range(ways):
                lend(band).start()

    for copy in local:
        copy.start()

    def to_peer(slab, step):
        peer = lax.rem(tensor_place + step, ways)
        return pltpu.make_async_remote_copy(
            src_ref=proj.at[slab, pl.ds(pl.multiple_of(peer * share, 8), share), :],
            dst_ref=landed.at[slab, step - 1],
            send_sem=sum_send.at[slab, step - 1], recv_sem=sum_recv.at[slab, step - 1],
            device_id={"tensor": peer}, device_id_type=mesh_ids,
        )

    def add_chunk(way, chunk, slab):
        if chunks[chunk] is None:
            proj[slab, :, 0:factor_rows] = contract(x_buf[...], in_buf[slab])
        else:
            begin, size = chunks[chunk]
            acc[way] += contract(g_buf[:, begin:begin + size], of_buf[slab, :, begin:begin + size])

    def send_sums(way, slab):
        proj[slab, :, factor_rows:2 * factor_rows] = acc[way]
        for step in range(1, ways):
            to_peer(slab, step).start()

    acc[...] = jnp.zeros_like(acc)
    for copy in local:
        copy.wait()
    for chunk in range(len(chunks)):
        if chunk < len(moved_chunks):
            @pl.when(jnp.logical_not(at_end))
            def _():
                add_chunk(0, chunk, place)
        else:
            add_chunk(0, chunk, place)
    send_sums(0, place)

    lane = lax.broadcasted_iota(jnp.int32, (1, LANES), 1)

    def pick(ids, base, into):
        def body(index, carry):
            number = ids[base + index]
            row = table_buf[pl.ds(lax.shift_right_logical(number, 7), 1), :]
            into[pl.ds(index, 1), :] = jnp.where(lane == jnp.bitwise_and(number, LANES - 1), row, 0.0)
            return carry
        return body

    lax.fori_loop(0, share, pick(ids_ref, tensor_place * share, tok_buf), 0)
    lax.fori_loop(0, queries, pick(query_ids_ref, 0, query_buf), 0)

    def arrive(step, carry):
        slabs = (place - 1 - step, place + 1 + step)
        acc[...] = jnp.zeros_like(acc)
        for chunk in range(len(chunks)):
            for way in range(2):
                @pl.when(takes(way, chunk, slabs[way]))
                def _():
                    hop(way, step, chunk, slabs[way]).wait_recv()

                    @pl.when(sends(way, chunk))
                    def _():
                        hop(way, step + 1, chunk, slabs[way]).start()

                    add_chunk(way, chunk, slabs[way])
                    if chunk == len(chunks) - 1:
                        send_sums(way, slabs[way])
        return carry

    lax.fori_loop(0, n - 1, arrive, 0)

    if moved:
        @pl.when(hosting)
        def _():
            for band in range(ways):
                lend(band).wait_recv()
                tokens = guest[band * share:(band + 1) * share, :]

                def pair(index, carry):
                    factors = of_buf[pl.ds(index * 2, 2), :, kept:hidden].reshape(2 * factor_rows, moved)
                    guest_proj[band, index] = contract(tokens, factors)
                    return carry

                lax.fori_loop(0, n // 2, pair, 0)
                hand_back(band, tensor_place).start()

    tok_weight = jnp.sum(tok_buf[...], axis=1, keepdims=True)
    query_weight = jnp.sum(query_buf[...], axis=1, keepdims=True)
    which = lax.broadcasted_iota(jnp.int32, (queries, LANES), 0)
    where = lax.broadcasted_iota(jnp.int32, (queries, LANES), 1)

    def finish(slab, scores):
        total = proj[slab, pl.ds(pl.multiple_of(tensor_place * share, 8), share), :]
        for step in range(1, ways):
            to_peer(slab, step).wait_recv()
            total = total + landed[slab, step - 1]
        proj[slab, pl.ds(pl.multiple_of(tensor_place * share, 8), share), :] = total
        return scores

    lax.fori_loop(0, n, finish, 0)

    if moved:
        @pl.when(at_end)
        def _():
            for source in range(ways):
                hand_back(tensor_place, source).wait_recv()

            def add_extra(slab, carry):
                pair = lax.div(slab, 2)
                more = extra[0, pair]
                for source in range(1, ways):
                    more = more + extra[source, pair]
                more = jnp.where(lax.rem(slab, 2) == 0, pltpu.roll(more, factor_rows, 1), more)
                rows = pl.ds(pl.multiple_of(tensor_place * share, 8), share)
                proj[slab, rows, :] += jnp.where(lane >= factor_rows, more, 0.0)
                return carry

            lax.fori_loop(0, n, add_extra, 0)

    def score(slab, scores):
        total = proj[slab, pl.ds(pl.multiple_of(tensor_place * share, 8), share), :]
        product = total * pltpu.roll(total, factor_rows, 1)
        first = which * rank_count - slab * factor_rows
        chosen = (where >= first) & (where < first + rank_count) & (where < factor_rows)
        chosen = chosen & (first >= 0)
        return scores + lax.dot_general(
            jnp.where(chosen, 1.0, 0.0), product * tok_weight, (((1,), (1,)), ((), ())),
            precision=lax.Precision.HIGHEST, preferred_element_type=jnp.float32,
        )

    scores = lax.fori_loop(0, n, score, jnp.zeros((queries, share), jnp.float32))
    scores_ref[...] = scores
    query_weight_ref[...] = jnp.broadcast_to(query_weight, scores.shape)

    def drain(step, carry):
        for chunk in range(len(chunks)):
            for way in range(2):
                slab = place - step if way == 0 else place + step
                @pl.when(sends(way, chunk) & ((slab >= 0) & (slab < n)))
                def _():
                    hop(way, step, chunk, slab).wait_send()
        for offset in range(1, ways):
            to_peer(step, offset).wait_send()
        return carry

    lax.fori_loop(0, n, drain, 0)

    if moved:
        @pl.when(at_end)
        def _():
            for band in range(ways):
                lend(band).wait_send()

        @pl.when(hosting)
        def _():
            for band in range(ways):
                hand_back(band, tensor_place).wait_send()


def solution(mesh):
    n, ways = mesh.shape["dp"], mesh.shape["tensor"]

    def shards(train_rows, out_grads, input_factor, output_factor, train_ids, query_ids, loss_weights):
        tokens, hidden = out_grads.shape
        factor_rows, width = input_factor.shape
        queries = query_ids.shape[0]
        share = tokens // ways
        moved = int(hidden // LANES * MOVED_PART) * LANES if n >= 4 and n % 2 == 0 else 0
        count = sum(len(part) for part in column_chunks(hidden, moved)) + 1
        rank_count = factor_rows * n // queries
        table = loss_weights.reshape(-1, LANES)
        anywhere = pl.BlockSpec(memory_space=pl.ANY)
        scalars = pl.BlockSpec(memory_space=pltpu.SMEM)
        dma = pltpu.SemaphoreType.DMA
        pairs = (ways, max(n // 2, 1), share, 2 * factor_rows)
        scores, query_weight = pl.pallas_call(
            functools.partial(kernel, n, ways, rank_count, moved),
            out_shape=[jax.ShapeDtypeStruct((queries, share), jnp.float32)] * 2,
            in_specs=[anywhere] * 5 + [scalars] * 2,
            out_specs=[pl.BlockSpec(memory_space=pltpu.VMEM)] * 2,
            scratch_shapes=[
                pltpu.VMEM((tokens, width), jnp.bfloat16),
                pltpu.VMEM((tokens, hidden), jnp.bfloat16),
                pltpu.VMEM((n, factor_rows, width), jnp.bfloat16),
                pltpu.VMEM((n, factor_rows, hidden), jnp.bfloat16),
                pltpu.VMEM(table.shape, jnp.float32),
                pltpu.VMEM((2, tokens, factor_rows), jnp.float32),
                pltpu.VMEM((n, tokens, 2 * factor_rows), jnp.float32),
                pltpu.VMEM((n, ways - 1, share, 2 * factor_rows), jnp.float32),
                pltpu.VMEM((share, LANES), jnp.float32),
                pltpu.VMEM((queries, LANES), jnp.float32),
                pltpu.VMEM((tokens, max(moved, LANES)), jnp.bfloat16),
                pltpu.VMEM(pairs, jnp.float32),
                pltpu.VMEM(pairs, jnp.float32),
                dma((5,)),
                dma((2, n)), dma((2, n)),
                dma((2, n, count)), dma((2, n, count)),
                dma((n, ways - 1)), dma((n, ways - 1)),
                dma((ways,)), dma((ways,)), dma((ways,)), dma((ways,)),
            ],
            compiler_params=pltpu.CompilerParams(
                collective_id=0, has_side_effects=True, vmem_limit_bytes=58 * 2**20
            ),
        )(train_rows, out_grads, input_factor, output_factor, table, train_ids, query_ids)
        return scores * query_weight

    return jax.shard_map(
        shards,
        mesh=mesh,
        in_specs=(
            P(("groups", "dp"), None),
            P(("groups", "dp"), "tensor"),
            P(("groups", "dp"), "tensor"),
            P(("groups", "dp"), "tensor"),
            P(("groups", "dp")),
            P("groups"),
            P(),
        ),
        out_specs=P(None, ("groups", "dp", "tensor")),
        check_vma=False,
    )
```
